32 devices in a mesh: az: 2 (over core), row: 16 (over z, y, x).
Axes of the slice: x: 2, y: 2, z: 4, core: 2. Of those that a mesh axis runs over, the one named last changes fastest.
Arguments:
- echoes: bfloat16 [2, 768, 16384], P(None, ('az', 'row')), may hold values from -6 to 6
- scaling_phase: bfloat16 [512, 16384], P('row'), may hold values from -3.140625 to 3.140625
- range_phase: bfloat16 [512, 16384], P('row'), may hold values from -3.140625 to 3.140625
- residual_phase: bfloat16 [512, 16384], P('row'), may hold values from -3.140625 to 3.140625
Outputs:
- focused: bfloat16 [2, 768, 16384], P(None, 'az', 'row')
The draws below stay inside these ranges and needn't reach their ends.
All inputs are finite; a program needn't handle non-finite values.
Results may differ from the reference program's by a relative error of at most 0.014.
Values may be sent and summed in bfloat16 or wider, within the bound.
A program may use at most 64 MiB of HBM per device.

```python
import math
import jax
import jax.numpy as jnp
from jax import lax

SAMPLES = 16384
SECTION_A = 128
AZ_SUB = 384
MARGIN = 128
AZ_LEN = 512
PULSES = 768
N_AZ = 2


def steps_of(key, shape, split, least, top_value):
    gain = 1.0
    for axis_at, blocks in split:
        heights = jax.random.uniform(jax.random.fold_in(jax.random.fold_in(key, 6), axis_at), (blocks,), jnp.float32, least / len(split), top_value / len(split))
        gain = gain * jnp.repeat(jnp.exp(heights), shape[axis_at] // blocks).reshape((-1,) + (1,) * (len(shape) - 1 - axis_at))
    return gain


def scatter_about(key, extent, spread, reach, split=(), kind=jnp.bfloat16):
    gain = steps_of(key, extent, split, -0.22, 0.18) if split else 1.0
    values = jax.random.normal(key, extent, jnp.float32) * spread * gain
    return jnp.minimum(jnp.maximum(values, -reach), reach).astype(kind)


def setup_inputs(seed: int = 0) -> dict:
    seeds = jax.random.split(jax.random.key(seed), 5)
    return {
        "echoes": scatter_about(seeds[0], (2, PULSES, SAMPLES), 1.0, 6.0, ((1, 32),)),
        "scaling_phase": jnp.clip(jax.random.uniform(seeds[1], (AZ_LEN, SAMPLES), jnp.float32, -3.140625, 3.140625), -3.140625, 3.140625).astype(jnp.bfloat16),
        "range_phase": jnp.clip(jax.random.uniform(seeds[2], (AZ_LEN, SAMPLES), jnp.float32, -3.140625, 3.140625), -3.140625, 3.140625).astype(jnp.bfloat16),
        "residual_phase": jnp.clip(jax.random.uniform(seeds[3], (AZ_LEN, SAMPLES), jnp.float32, -3.140625, 3.140625), -3.140625, 3.140625).astype(jnp.bfloat16),
    }


def transform_table(length, rotation):
    indices = jnp.arange(length, dtype=jnp.int32)
    product = indices[:, None] * indices[None, :] % length
    angles = product.astype(jnp.float32) * (2.0 * math.pi / length)
    factor = 1.0 / math.sqrt(length)
    real_half = (jnp.cos(angles) * factor).astype(jnp.bfloat16)
    imaginary = (rotation * jnp.sin(angles) * factor).astype(jnp.bfloat16)
    return (real_half, imaginary)

def complex_einsum(formula, values, table_real, table_imag):
    first_part = values[0].astype(jnp.float32)
    second_part = values[1].astype(jnp.float32)
    table_real = table_real.astype(jnp.float32)
    table_imag = table_imag.astype(jnp.float32)
    real_half = jnp.einsum(formula, first_part, table_real, precision=lax.Precision.HIGHEST) - jnp.einsum(formula, second_part, table_imag, precision=lax.Precision.HIGHEST)
    imaginary = jnp.einsum(formula, first_part, table_imag, precision=lax.Precision.HIGHEST) + jnp.einsum(formula, second_part, table_real, precision=lax.Precision.HIGHEST)
    return jnp.stack([real_half, imaginary])

def rotate(values, angles):
    cosine = jnp.cos(angles)
    sine_part = jnp.sin(angles)
    return jnp.stack([values[0] * cosine - values[1] * sine_part, values[0] * sine_part + values[1] * cosine])

def first_section(row_data, rotation):
    row_count = row_data.shape[1]
    length = row_data.shape[2]
    section_b = length // SECTION_A
    grid_view = row_data.reshape(2, row_count, SECTION_A, section_b)
    table_real, table_imag = transform_table(SECTION_A, rotation)
    mixed_sum = complex_einsum('rab,ak->rkb', grid_view, table_real, table_imag)
    low_index = jnp.arange(SECTION_A, dtype=jnp.int32)[:, None]
    high_index = jnp.arange(section_b, dtype=jnp.int32)[None, :]
    angles = (low_index * high_index % length).astype(jnp.float32) * (rotation * 2.0 * math.pi / length)
    return rotate(mixed_sum, angles).astype(jnp.bfloat16)

def second_section(half_done, rotation, phases):
    row_count = half_done.shape[1]
    section_b = half_done.shape[3]
    table_real, table_imag = transform_table(section_b, rotation)
    mixed_sum = complex_einsum('rkb,bm->rmk', half_done, table_real, table_imag)
    flattened = mixed_sum.reshape(2, row_count, SECTION_A * section_b)
    return rotate(flattened, phases.astype(jnp.float32)).astype(jnp.bfloat16)

def reference(echoes, scaling_phase, range_phase, residual_phase):
    blocks = echoes.reshape(2, N_AZ, AZ_SUB, SAMPLES)
    following = jnp.concatenate([blocks[:, 1:, :MARGIN, :], jnp.zeros((2, 1, MARGIN, SAMPLES), jnp.bfloat16)], axis=1)
    extended = jnp.concatenate([blocks, following], axis=2)

    def focus_block(block_data):
        forward_real, forward_imag = transform_table(AZ_LEN, -1.0)
        spectrum = complex_einsum('mr,mf->fr', block_data, forward_real, forward_imag).astype(jnp.bfloat16)
        spectrum = lax.optimization_barrier(spectrum)
        scaled = rotate(spectrum.astype(jnp.float32), scaling_phase.astype(jnp.float32)).astype(jnp.bfloat16)
        compressed = second_section(first_section(scaled, -1.0), -1.0, range_phase)
        restored = second_section(first_section(compressed, 1.0), 1.0, residual_phase)
        backward_real, backward_imag = transform_table(AZ_LEN, 1.0)
        result = complex_einsum('fr,fm->mr', restored, backward_real[:, :AZ_SUB], backward_imag[:, :AZ_SUB])
        return result.astype(jnp.bfloat16)
    images = lax.map(focus_block, jnp.moveaxis(extended, 1, 0))
    return jnp.moveaxis(images, 0, 1).reshape(2, PULSES, SAMPLES)
```

```python
import functools
import math

import jax
import jax.numpy as jnp
import ml_dtypes
import numpy as np
from jax import lax
from jax.experimental import pallas as pl
from jax.experimental.pallas import tpu as pltpu
from jax.sharding import PartitionSpec as P

SECTION_A = 128
MARGIN = 128
FG = 8
MESH = pl.DeviceIdType.MESH
F32 = jnp.float32
BF16 = jnp.bfloat16


def dft_table(length, rotation):
    indices = np.arange(length)
    angles = (indices[:, None] * indices[None, :] % length) * (2.0 * math.pi / length)
    factor = 1.0 / math.sqrt(length)
    rounded = lambda values: values.astype(ml_dtypes.bfloat16).astype(np.float32)
    return rounded(np.cos(angles) * factor), rounded(rotation * np.sin(angles) * factor)


def tables(n, pulses, rows, margin_blocks, block, per_device):
    length = block + MARGIN
    groups = per_device // FG
    freq = np.arange(length).reshape(n, groups, FG).transpose(1, 0, 2)
    real, imag = dft_table(length, -1.0)
    sources = n + margin_blocks
    forward = np.zeros((groups, n, 2, FG, sources, rows), np.float32)
    for s in range(sources):
        first = s * pulses if s < n else block + (s - n) * pulses
        count = min(pulses, (block if s < n else length) - first)
        m = first + np.arange(count)
        wr = real[m][:, freq].transpose(1, 2, 3, 0)
        wi = imag[m][:, freq].transpose(1, 2, 3, 0)
        forward[:, :, 0, :, s, :count] = wr
        forward[:, :, 0, :, s, pulses : pulses + count] = -wi
        forward[:, :, 1, :, s, :count] = wi
        forward[:, :, 1, :, s, pulses : pulses + count] = wr
    forward = forward.reshape(groups, n * 2 * FG, sources * rows)
    real, imag = dft_table(length, 1.0)
    backward = np.zeros((2, block, groups, n, 2, FG), np.float32)
    wr, wi = real[:block][:, freq], imag[:block][:, freq]
    backward[0, :, :, :, 0], backward[0, :, :, :, 1] = wr, -wi
    backward[1, :, :, :, 0], backward[1, :, :, :, 1] = wi, wr
    backward = backward.reshape(2 * block, groups * n * 2 * FG)
    sections = []
    for rotation in (-1.0, 1.0):
        real, imag = dft_table(SECTION_A, rotation)
        sections.append(np.block([[real, -imag], [imag, real]]))
        sections.append(np.block([[real, imag], [-imag, real]]))
    index = np.arange(SECTION_A)
    angles = index[:, None] * index[None, :] * (2.0 * math.pi / SECTION_A**2)
    twiddle = np.stack([np.cos(angles), np.sin(angles)]).astype(np.float32)
    as_bf16 = lambda values: values.astype(ml_dtypes.bfloat16)
    return as_bf16(forward), as_bf16(backward), as_bf16(np.stack(sections)), twiddle


def cos_sin(x):
    h = x * 0.5
    q = h * h
    s = 1.0 / 362880.0
    for c in (-1.0 / 5040.0, 1.0 / 120.0, -1.0 / 6.0, 1.0):
        s = s * q + c
    s = s * h
    k = -1.0 / 3628800.0
    for c in (1.0 / 40320.0, -1.0 / 720.0, 1.0 / 24.0, -0.5, 1.0):
        k = k * q + c
    return 1.0 - 2.0 * s * s, 2.0 * s * k


def kernel(
    n, n_az, margin_blocks, groups, rc,
    echoes, scaling, rng, residual, forward, backward, sections, twiddle,
    out,
    recv1, spec, recv2, send3, recv3, ph, sc_t, rg_t, rs_t, xs,
    s1, r1, s2, r2, l2, s3, r3, l3, pm, ms, mr,
):
    a, me = lax.axis_index("az"), lax.axis_index("row")
    lane_tiles = rc // 128
    order = sorted(range(1, n), key=lambda i: abs(i - n // 2))

    def peer(i):
        return lax.rem(me + i, n)

    barrier = pltpu.get_barrier_semaphore()
    for i in range(1, n):
        pl.semaphore_signal(barrier, inc=1, device_id={"row": peer(i)}, device_id_type=MESH)

    steps = sorted({1, n_az - 1})
    for step in steps:
        beside = lax.rem(a + step, n_az)
        pl.semaphore_signal(barrier, inc=1, device_id={"az": beside}, device_id_type=MESH)
    pl.semaphore_wait(barrier, n - 1 + len(steps))

    def columns(d):
        return pl.ds(pl.multiple_of(d * rc, 128), rc)

    for i in order:
        d = peer(i)
        pltpu.make_async_remote_copy(
            src_ref=echoes.at[:, columns(d)], dst_ref=recv1.at[me], send_sem=s1,
            recv_sem=r1.at[me], device_id={"row": d}, device_id_type=MESH,
        ).start()
    pltpu.make_async_copy(echoes.at[:, columns(me)], recv1.at[me], r1.at[me]).start()
    for k, phase in enumerate((scaling, rng, residual)):
        pltpu.make_async_copy(phase, ph.at[k], pm.at[k]).start()

    @pl.when(a == n_az - 1)
    def _():
        for j in range(margin_blocks):
            recv1[n + j] = jnp.zeros(recv1.shape[1:], BF16)

    for k, phase in enumerate((scaling, rng, residual)):
        pltpu.make_async_copy(phase, ph.at[k], pm.at[k]).wait()
    for k, table in ((0, sc_t), (2, rs_t)):
        for pair in range(groups // 2):

            def natural(d, carry, k=k, table=table, pair=pair):
                x = ph[k, pl.ds(pair * 2 * FG, 2 * FG), columns(d)].astype(F32)
                c, s = cos_sin(x)
                for h in range(2):
                    table[2 * pair + h, d, 0] = c[h * FG : (h + 1) * FG]
                    table[2 * pair + h, d, 1] = s[h * FG : (h + 1) * FG]
                return carry

            lax.fori_loop(0, n, natural, 0)
    for pair in range(groups // 2):

        def spread(d, carry, pair=pair):
            x = ph[1, pl.ds(pair * 2 * FG, 2 * FG), columns(d)].astype(F32)
            for j in range(lane_tiles):
                at = pl.ds(pl.multiple_of((d * lane_tiles + j) * FG, FG), FG)
                for h in range(2):
                    xs[h, at, :] = x[h * FG : (h + 1) * FG, j * 128 : (j + 1) * 128]
            return carry

        lax.fori_loop(0, n, spread, 0)
        for h in range(2):
            for f in range(FG):
                c, s = cos_sin(xs[h, pl.ds(f, 128, stride=FG), :].T)
                rg_t[2 * pair + h, f, 0] = c
                rg_t[2 * pair + h, f, 1] = s

    def arrived(s):
        pltpu.make_async_copy(echoes.at[:, pl.ds(0, rc)], recv1.at[s], r1.at[s]).wait()

    def margin_copy():
        return pltpu.make_async_remote_copy(
            src_ref=recv1.at[pl.ds(0, margin_blocks)],
            dst_ref=recv1.at[pl.ds(n, margin_blocks)],
            send_sem=ms, recv_sem=mr,
            device_id={"az": a - 1}, device_id_type=MESH,
        )

    for s in range(margin_blocks):
        arrived(s)

    @pl.when(a > 0)
    def _():
        margin_copy().start()

    for s in range(margin_blocks, n):
        arrived(s)

    @pl.when(a < n_az - 1)
    def _():
        pltpu.make_async_copy(
            recv1.at[pl.ds(0, margin_blocks)], recv1.at[pl.ds(n, margin_blocks)], mr
        ).wait()

    def send_group(source, target, g, send_sem, recv_sem, local_sem):
        for i in order:
            d = peer(i)
            pltpu.make_async_remote_copy(
                src_ref=source.at[g, d], dst_ref=target.at[g, me], send_sem=send_sem.at[g],
                recv_sem=recv_sem.at[g], device_id={"row": d}, device_id_type=MESH,
            ).start()
        pltpu.make_async_copy(source.at[g, me], target.at[g, me], local_sem.at[g]).start()

    def group_wait(source, target, g, sem):
        some = pl.ds(0, n - 1)
        pltpu.make_async_copy(source.at[g, some], target.at[g, some], sem.at[g]).wait()

    def group_arrived(source, target, g, recv_sem, local_sem):
        group_wait(source, target, g, recv_sem)
        pltpu.make_async_copy(source.at[g, me], target.at[g, me], local_sem.at[g]).wait()

    depth = recv1.shape[0] * recv1.shape[1]

    def azimuth(g, carry):
        total = jnp.dot(forward[g], recv1[...].reshape(depth, rc), preferred_element_type=F32)
        spec[g] = total.astype(BF16).reshape(n, 2 * FG, rc)
        send_group(spec, recv2, g, s2, r2, l2)
        return carry

    lax.fori_loop(0, groups, azimuth, 0)

    def part(values, f):
        return values[:, f * 128 : (f + 1) * 128]

    def range_group(g, carry):
        group_arrived(spec, recv2, g, r2, l2)

        def scale(d, inner):
            block = recv2[g, d].astype(F32)
            re, im = block[:FG], block[FG:]
            c, s = sc_t[g, d, 0], sc_t[g, d, 1]
            x, y = re * c - im * s, re * s + im * c
            for j in range(lane_tiles):
                at = pl.ds(pl.multiple_of((d * lane_tiles + j) * FG, FG), FG)
                xs[0, at, :] = part(x, j)
                xs[1, at, :] = part(y, j)
            return inner

        lax.fori_loop(0, n, scale, 0)
        tc, ts = twiddle[0], twiddle[1]
        v = jnp.concatenate(
            [
                jnp.concatenate(
                    [xs[c, pl.ds(f, 128, stride=FG), :].astype(BF16) for f in range(FG)], axis=1
                )
                for c in range(2)
            ],
            axis=0,
        )
        y = jnp.dot(sections[0], v, preferred_element_type=F32)
        half = []
        for f in range(FG):
            re, im = part(y[:128], f), part(y[128:], f)
            half.append(jnp.concatenate([re * tc + im * ts, im * tc - re * ts], axis=1).astype(BF16))
        z = jnp.dot(jnp.concatenate(half, axis=0), sections[1], preferred_element_type=F32)
        squeezed = []
        for f in range(FG):
            rows = z[f * 128 : (f + 1) * 128]
            re, im = rows[:, :128], rows[:, 128:]
            c, s = rg_t[g, f, 0], rg_t[g, f, 1]
            squeezed.append(jnp.concatenate([re * c - im * s, re * s + im * c], axis=1).astype(BF16))
        u = jnp.dot(jnp.concatenate(squeezed, axis=0), sections[3], preferred_element_type=F32)
        reals, imags = [], []
        for f in range(FG):
            rows = u[f * 128 : (f + 1) * 128]
            re, im = rows[:, :128], rows[:, 128:]
            reals.append((re * tc - im * ts).astype(BF16))
            imags.append((re * ts + im * tc).astype(BF16))
        q = jnp.concatenate(
            [jnp.concatenate(reals, axis=1), jnp.concatenate(imags, axis=1)], axis=0
        )
        w = jnp.dot(sections[2], q, preferred_element_type=F32)
        for f in range(FG):
            xs[0, pl.ds(f, 128, stride=FG), :] = part(w[:128], f)
            xs[1, pl.ds(f, 128, stride=FG), :] = part(w[128:], f)

        def finish(d, inner):
            res, ims = [], []
            for j in range(lane_tiles):
                at = pl.ds(pl.multiple_of((d * lane_tiles + j) * FG, FG), FG)
                res.append(xs[0, at, :])
                ims.append(xs[1, at, :])
            re, im = jnp.concatenate(res, axis=1), jnp.concatenate(ims, axis=1)
            c, s = rs_t[g, d, 0], rs_t[g, d, 1]
            send3[g, d] = jnp.concatenate([re * c - im * s, re * s + im * c], axis=0).astype(BF16)
            return inner

        lax.fori_loop(0, n, finish, 0)
        send_group(send3, recv3, g, s3, r3, l3)
        return carry

    lax.fori_loop(0, groups, range_group, 0)

    for g in range(groups):
        group_arrived(send3, recv3, g, r3, l3)
    out[...] = jnp.dot(
        backward[...], recv3[...].reshape(groups * n * 2 * FG, rc), preferred_element_type=F32
    ).astype(BF16)

    for g in range(groups):
        group_wait(spec, recv2, g, s2)
        group_wait(send3, recv3, g, s3)
    some = pl.ds(0, n - 1)
    pltpu.make_async_copy(recv1.at[some], recv1.at[some], s1).wait()

    @pl.when(a > 0)
    def _():
        margin_copy().wait_send()


def on_device(n_az, n, echoes, scaling_phase, range_phase, residual_phase):
    _, pulses, length = echoes.shape
    per_device = scaling_phase.shape[0]
    rc = length // n
    block = pulses * n
    rows = -(-2 * pulses // 16) * 16
    margin_blocks = -(-MARGIN // pulses)
    groups = per_device // FG
    stacked = echoes.reshape(2 * pulses, length)
    if rows > 2 * pulses:
        stacked = jnp.pad(stacked, ((0, rows - 2 * pulses), (0, 0)))
    forward, backward, sections, twiddle = tables(n, pulses, rows, margin_blocks, block, per_device)
    anywhere = pl.BlockSpec(memory_space=pl.ANY)
    vmem = pl.BlockSpec(memory_space=pltpu.VMEM)
    exchange = pltpu.VMEM((groups, n, 2 * FG, rc), BF16)
    dma = pltpu.SemaphoreType.DMA
    result = pl.pallas_call(
        functools.partial(kernel, n, n_az, margin_blocks, groups, rc),
        out_shape=jax.ShapeDtypeStruct((2 * block, rc), BF16),
        in_specs=[anywhere] * 4 + [vmem] * 4,
        out_specs=vmem,
        scratch_shapes=[
            pltpu.VMEM((n + margin_blocks, rows, rc), BF16),
            exchange, exchange, exchange, exchange,
            pltpu.VMEM((3, per_device, length), BF16),
            pltpu.VMEM((groups, n, 2, FG, rc), F32),
            pltpu.VMEM((groups, FG, 2, 128, 128), F32),
            pltpu.VMEM((groups, n, 2, FG, rc), F32),
            pltpu.VMEM((2, 128 * FG, 128), F32),
            dma, dma((n,)), dma((groups,)), dma((groups,)), dma((groups,)),
            dma((groups,)), dma((groups,)), dma((groups,)), dma((3,)), dma, dma,
        ],
        compiler_params=pltpu.CompilerParams(
            collective_id=0, has_side_effects=True, vmem_limit_bytes=56 * 1024 * 1024
        ),
    )(
        stacked, scaling_phase, range_phase, residual_phase,
        jnp.asarray(forward), jnp.asarray(backward), jnp.asarray(sections), jnp.asarray(twiddle),
    )
    return result.reshape(2, block, rc)


def solution(mesh):
    placed = (P(None, ("az", "row"), None), P("row", None), P("row", None), P("row", None))
    return jax.shard_map(
        functools.partial(on_device, mesh.shape["az"], mesh.shape["row"]),
        mesh=mesh, in_specs=placed, out_specs=P(None, "az", "row"), check_vma=False,
    )
```

```python
import functools
import math

import jax
import jax.numpy as jnp
import ml_dtypes
import numpy as np
from jax import lax
from jax.experimental import pallas as pl
from jax.experimental.pallas import tpu as pltpu
from jax.sharding import PartitionSpec as P

SECTION_A = 128
MARGIN = 128
FG = 8
CHUNKS = 2
MESH = pl.DeviceIdType.MESH
F32 = jnp.float32
BF16 = jnp.bfloat16


def dft_table(length, rotation):
    indices = np.arange(length)
    angles = (indices[:, None] * indices[None, :] % length) * (2.0 * math.pi / length)
    factor = 1.0 / math.sqrt(length)
    rounded = lambda values: values.astype(ml_dtypes.bfloat16).astype(np.float32)
    return rounded(np.cos(angles) * factor), rounded(rotation * np.sin(angles) * factor)


def tables(n, pulses, rows, margin_blocks, block, per_device):
    length = block + MARGIN
    groups = per_device // FG
    freq = np.arange(length).reshape(n, groups, FG).transpose(1, 0, 2)
    real, imag = dft_table(length, -1.0)
    sources = n + margin_blocks
    forward = np.zeros((groups, n, 2, FG, sources, rows), np.float32)
    for s in range(sources):
        first = s * pulses if s < n else block + (s - n) * pulses
        count = min(pulses, (block if s < n else length) - first)
        m = first + np.arange(count)
        wr = real[m][:, freq].transpose(1, 2, 3, 0)
        wi = imag[m][:, freq].transpose(1, 2, 3, 0)
        forward[:, :, 0, :, s, :count] = wr
        forward[:, :, 0, :, s, pulses : pulses + count] = -wi
        forward[:, :, 1, :, s, :count] = wi
        forward[:, :, 1, :, s, pulses : pulses + count] = wr
    forward = forward.reshape(groups, n * 2 * FG, sources * rows)
    real, imag = dft_table(length, 1.0)
    backward = np.zeros((2, block, groups, n, 2, FG), np.float32)
    wr, wi = real[:block][:, freq], imag[:block][:, freq]
    backward[0, :, :, :, 0], backward[0, :, :, :, 1] = wr, -wi
    backward[1, :, :, :, 0], backward[1, :, :, :, 1] = wi, wr
    backward = backward.reshape(2 * block, groups, n * 2 * FG).transpose(1, 0, 2)
    sections = []
    for rotation in (-1.0, 1.0):
        real, imag = dft_table(SECTION_A, rotation)
        sections.append(np.block([[real, -imag], [imag, real]]))
        sections.append(np.block([[real, imag], [-imag, real]]))
    index = np.arange(SECTION_A)
    angles = index[:, None] * index[None, :] * (2.0 * math.pi / SECTION_A**2)
    twiddle = np.stack([np.cos(angles), np.sin(angles)]).astype(np.float32)
    as_bf16 = lambda values: values.astype(ml_dtypes.bfloat16)
    return as_bf16(forward), as_bf16(backward), as_bf16(np.stack(sections)), twiddle


def cos_sin(x):
    h = x * 0.5
    q = h * h
    s = 1.0 / 362880.0
    for c in (-1.0 / 5040.0, 1.0 / 120.0, -1.0 / 6.0, 1.0):
        s = s * q + c
    s = s * h
    k = -1.0 / 3628800.0
    for c in (1.0 / 40320.0, -1.0 / 720.0, 1.0 / 24.0, -0.5, 1.0):
        k = k * q + c
    return 1.0 - 2.0 * s * s, 2.0 * s * k


def kernel(
    n, n_az, margin_blocks, groups, rc,
    echoes, scaling, rng, residual, forward_in, backward_in, sections_in, twiddle_in,
    out,
    recv1, spec, recv2, send3, recv3, ph, sc_t, rg_t, rs_t, xs, total_back,
    forward, backward, sections, twiddle,
    s1, r1, s2, r2, l2, s3, r3, l3, pm, ms, mr, tm,
):
    a, me = lax.axis_index("az"), lax.axis_index("row")
    lane_tiles, cw = rc // 128, rc // CHUNKS
    half_row = n // 2
    side, place = lax.div(me, half_row), lax.rem(me, half_row)
    order = [(1, 0)]
    for i in range(1, half_row):
        order += [(0, i), (1, i)]

    def peer(partner):
        other, i = partner
        there = 1 - side if other else side
        return there * half_row + lax.rem(place + i, half_row)

    barrier = pltpu.get_barrier_semaphore()
    for i in order:
        pl.semaphore_signal(barrier, inc=1, device_id={"row": peer(i)}, device_id_type=MESH)

    steps = sorted({1, n_az - 1})
    for step in steps:
        beside = lax.rem(a + step, n_az)
        pl.semaphore_signal(barrier, inc=1, device_id={"az": beside}, device_id_type=MESH)
    pl.semaphore_wait(barrier, n - 1 + len(steps))

    def columns(d):
        return pl.ds(pl.multiple_of(d * rc, 128), rc)

    def chunk_columns(d, ch):
        return pl.ds(pl.multiple_of(d * rc + ch * cw, 128), cw)

    for ch in range(CHUNKS):
        for i in order:
            d = peer(i)
            pltpu.make_async_remote_copy(
                src_ref=echoes.at[:, chunk_columns(d, ch)], dst_ref=recv1.at[ch, me],
                send_sem=s1.at[ch], recv_sem=r1.at[ch, me],
                device_id={"row": d}, device_id_type=MESH,
            ).start()
        pltpu.make_async_copy(
            echoes.at[:, chunk_columns(me, ch)], recv1.at[ch, me], r1.at[ch, me]
        ).start()
    loads = [pltpu.make_async_copy(p, ph.at[k], pm.at[k]) for k, p in enumerate((scaling, rng, residual))]
    fixed = ((forward_in, forward), (twiddle_in, twiddle), (sections_in, sections), (backward_in, backward))
    loads += [pltpu.make_async_copy(x, y, tm.at[k]) for k, (x, y) in enumerate(fixed)]
    for k in (0, 3, 1, 2, 4, 5, 6):
        loads[k].start()

    @pl.when(a == n_az - 1)
    def _():
        for ch in range(CHUNKS):
            for j in range(margin_blocks):
                recv1[ch, n + j] = jnp.zeros(recv1.shape[2:], BF16)

    def natural_table(k, table):
        loads[k].wait()

        def natural(step, carry):
            pair, d = lax.div(step, n), lax.rem(step, n)
            rows = pl.ds(pl.multiple_of(pair * 2 * FG, 2 * FG), 2 * FG)
            c, s = cos_sin(ph[k, rows, columns(d)].astype(F32))
            for h in range(2):
                table[2 * pair + h, d, 0] = c[h * FG : (h + 1) * FG]
                table[2 * pair + h, d, 1] = s[h * FG : (h + 1) * FG]
            return carry

        lax.fori_loop(0, n * (groups // 2), natural, 0)

    def turned_table():
        loads[1].wait()

        def turn(pair, carry):
            rows = pl.ds(pl.multiple_of(pair * 2 * FG, 2 * FG), 2 * FG)

            def spread(d, inner):
                x = ph[1, rows, columns(d)].astype(F32)
                for j in range(lane_tiles):
                    at = pl.ds(pl.multiple_of((d * lane_tiles + j) * FG, FG), FG)
                    for h in range(2):
                        xs[h, at, :] = x[h * FG : (h + 1) * FG, j * 128 : (j + 1) * 128]
                return inner

            lax.fori_loop(0, n, spread, 0)
            for h in range(2):
                for f in range(FG):
                    c, s = cos_sin(xs[h, pl.ds(f, 128, stride=FG), :].T)
                    rg_t[2 * pair + h, f, 0] = c
                    rg_t[2 * pair + h, f, 1] = s
            return carry

        lax.fori_loop(0, groups // 2, turn, 0)

    def arrived(ch, s):
        pltpu.make_async_copy(echoes.at[:, pl.ds(0, cw)], recv1.at[ch, s], r1.at[ch, s]).wait()

    def margin_copy(ch):
        return pltpu.make_async_remote_copy(
            src_ref=recv1.at[ch, pl.ds(0, margin_blocks)],
            dst_ref=recv1.at[ch, pl.ds(n, margin_blocks)],
            send_sem=ms.at[ch], recv_sem=mr.at[ch],
            device_id={"az": a - 1}, device_id_type=MESH,
        )

    def send_group(source, target, at, send_sem, recv_sem, local_sem):
        for i in order:
            d = peer(i)
            pltpu.make_async_remote_copy(
                src_ref=source.at[(*at, d)], dst_ref=target.at[(*at, me)], send_sem=send_sem.at[at],
                recv_sem=recv_sem.at[at], device_id={"row": d}, device_id_type=MESH,
            ).start()
        pltpu.make_async_copy(
            source.at[(*at, me)], target.at[(*at, me)], local_sem.at[at]
        ).start()

    def group_wait(source, target, at, sem):
        some = pl.ds(0, n - 1)
        pltpu.make_async_copy(source.at[(*at, some)], target.at[(*at, some)], sem.at[at]).wait()

    def group_arrived(source, target, at, recv_sem, local_sem):
        group_wait(source, target, at, recv_sem)
        pltpu.make_async_copy(source.at[(*at, me)], target.at[(*at, me)], local_sem.at[at]).wait()

    depth = recv1.shape[1] * recv1.shape[2]

    def azimuth_chunk(ch):
        for s in range(margin_blocks):
            arrived(ch, s)

        @pl.when(a > 0)
        def _():
            margin_copy(ch).start()

        for s in range(margin_blocks, n):
            arrived(ch, s)

        @pl.when(a < n_az - 1)
        def _():
            pltpu.make_async_copy(
                recv1.at[ch, pl.ds(0, margin_blocks)], recv1.at[ch, pl.ds(n, margin_blocks)],
                mr.at[ch],
            ).wait()

        def azimuth(g, carry):
            total = jnp.dot(
                forward[g], recv1[ch].reshape(depth, cw), preferred_element_type=F32
            )
            spec[g, ch] = total.astype(BF16).reshape(n, 2 * FG, cw)
            send_group(spec, recv2, (g, ch), s2, r2, l2)
            return carry

        lax.fori_loop(0, groups, azimuth, 0)

    natural_table(0, sc_t)
    loads[3].wait()
    azimuth_chunk(0)
    turned_table()
    azimuth_chunk(1)
    natural_table(2, rs_t)
    for k in (4, 5, 6):
        loads[k].wait()

    def part(values, f):
        return values[:, f * 128 : (f + 1) * 128]

    def range_group(g, carry):
        for ch in range(CHUNKS):
            group_arrived(spec, recv2, (g, ch), r2, l2)

        def scale(d, inner):
            block = jnp.concatenate([recv2[g, ch, d] for ch in range(CHUNKS)], axis=1).astype(F32)
            re, im = block[:FG], block[FG:]
            c, s = sc_t[g, d, 0], sc_t[g, d, 1]
            x, y = re * c - im * s, re * s + im * c
            for j in range(lane_tiles):
                at = pl.ds(pl.multiple_of((d * lane_tiles + j) * FG, FG), FG)
                xs[0, at, :] = part(x, j)
                xs[1, at, :] = part(y, j)
            return inner

        lax.fori_loop(0, n, scale, 0)
        tc, ts = twiddle[0], twiddle[1]
        v = jnp.concatenate(
            [
                jnp.concatenate(
                    [xs[c, pl.ds(f, 128, stride=FG), :].astype(BF16) for f in range(FG)], axis=1
                )
                for c in range(2)
            ],
            axis=0,
        )
        y = jnp.dot(sections[0], v, preferred_element_type=F32)
        half = []
        for f in range(FG):
            re, im = part(y[:128], f), part(y[128:], f)
            half.append(jnp.concatenate([re * tc + im * ts, im * tc - re * ts], axis=1).astype(BF16))
        z = jnp.dot(jnp.concatenate(half, axis=0), sections[1], preferred_element_type=F32)
        squeezed = []
        for f in range(FG):
            rows = z[f * 128 : (f + 1) * 128]
            re, im = rows[:, :128], rows[:, 128:]
            c, s = rg_t[g, f, 0], rg_t[g, f, 1]
            squeezed.append(jnp.concatenate([re * c - im * s, re * s + im * c], axis=1).astype(BF16))
        u = jnp.dot(jnp.concatenate(squeezed, axis=0), sections[3], preferred_element_type=F32)
        reals, imags = [], []
        for f in range(FG):
            rows = u[f * 128 : (f + 1) * 128]
            re, im = rows[:, :128], rows[:, 128:]
            reals.append((re * tc - im * ts).astype(BF16))
            imags.append((re * ts + im * tc).astype(BF16))
        q = jnp.concatenate(
            [jnp.concatenate(reals, axis=1), jnp.concatenate(imags, axis=1)], axis=0
        )
        w = jnp.dot(sections[2], q, preferred_element_type=F32)
        for f in range(FG):
            xs[0, pl.ds(f, 128, stride=FG), :] = part(w[:128], f)
            xs[1, pl.ds(f, 128, stride=FG), :] = part(w[128:], f)

        def finish(d, inner):
            res, ims = [], []
            for j in range(lane_tiles):
                at = pl.ds(pl.multiple_of((d * lane_tiles + j) * FG, FG), FG)
                res.append(xs[0, at, :])
                ims.append(xs[1, at, :])
            re, im = jnp.concatenate(res, axis=1), jnp.concatenate(ims, axis=1)
            c, s = rs_t[g, d, 0], rs_t[g, d, 1]
            send3[g, d] = jnp.concatenate([re * c - im * s, re * s + im * c], axis=0).astype(BF16)
            return inner

        lax.fori_loop(0, n, finish, 0)
        send_group(send3, recv3, (g,), s3, r3, l3)
        return carry

    lax.fori_loop(0, groups, range_group, 0)

    for g in range(groups):
        group_arrived(send3, recv3, (g,), r3, l3)
        term = jnp.dot(
            backward[g], recv3[g].reshape(n * 2 * FG, rc), preferred_element_type=F32
        )
        if g > 0:
            term = total_back[...] + term
        if g < groups - 1:
            total_back[...] = term
        else:
            out[...] = term.astype(BF16)

    for g in range(groups):
        for ch in range(CHUNKS):
            group_wait(spec, recv2, (g, ch), s2)
        group_wait(send3, recv3, (g,), s3)
    some = pl.ds(0, n - 1)
    for ch in range(CHUNKS):
        pltpu.make_async_copy(recv1.at[ch, some], recv1.at[ch, some], s1.at[ch]).wait()

        @pl.when(a > 0)
        def _(ch=ch):
            margin_copy(ch).wait_send()


def on_device(n_az, n, echoes, scaling_phase, range_phase, residual_phase):
    _, pulses, length = echoes.shape
    per_device = scaling_phase.shape[0]
    rc = length // n
    block = pulses * n
    rows = -(-2 * pulses // 16) * 16
    margin_blocks = -(-MARGIN // pulses)
    groups = per_device // FG
    stacked = echoes.reshape(2 * pulses, length)
    if rows > 2 * pulses:
        stacked = jnp.pad(stacked, ((0, rows - 2 * pulses), (0, 0)))
    forward, backward, sections, twiddle = tables(n, pulses, rows, margin_blocks, block, per_device)
    anywhere = pl.BlockSpec(memory_space=pl.ANY)
    vmem = pl.BlockSpec(memory_space=pltpu.VMEM)
    exchange = pltpu.VMEM((groups, n, 2 * FG, rc), BF16)
    chunked = pltpu.VMEM((groups, CHUNKS, n, 2 * FG, rc // CHUNKS), BF16)
    dma = pltpu.SemaphoreType.DMA
    result = pl.pallas_call(
        functools.partial(kernel, n, n_az, margin_blocks, groups, rc),
        out_shape=jax.ShapeDtypeStruct((2 * block, rc), BF16),
        in_specs=[anywhere] * 8,
        out_specs=vmem,
        scratch_shapes=[
            pltpu.VMEM((CHUNKS, n + margin_blocks, rows, rc // CHUNKS), BF16),
            chunked, chunked, exchange, exchange,
            pltpu.VMEM((3, per_device, length), BF16),
            pltpu.VMEM((groups, n, 2, FG, rc), F32),
            pltpu.VMEM((groups, FG, 2, 128, 128), F32),
            pltpu.VMEM((groups, n, 2, FG, rc), F32),
            pltpu.VMEM((2, 128 * FG, 128), F32),
            pltpu.VMEM((2 * block, rc), F32),
            *[pltpu.VMEM(t.shape, t.dtype) for t in (forward, backward, sections, twiddle)],
            dma((CHUNKS,)), dma((CHUNKS, n)),
            dma((groups, CHUNKS)), dma((groups, CHUNKS)), dma((groups, CHUNKS)),
            dma((groups,)), dma((groups,)), dma((groups,)),
            dma((3,)), dma((CHUNKS,)), dma((CHUNKS,)), dma((4,)),
        ],
        compiler_params=pltpu.CompilerParams(
            collective_id=0, has_side_effects=True, vmem_limit_bytes=56 * 1024 * 1024
        ),
    )(
        stacked, scaling_phase, range_phase, residual_phase,
        jnp.asarray(forward), jnp.asarray(backward), jnp.asarray(sections), jnp.asarray(twiddle),
    )
    return result.reshape(2, block, rc)


def solution(mesh):
    placed = (P(None, ("az", "row"), None), P("row", None), P("row", None), P("row", None))
    return jax.shard_map(
        functools.partial(on_device, mesh.shape["az"], mesh.shape["row"]),
        mesh=mesh, in_specs=placed, out_specs=P(None, "az", "row"), check_vma=False,
    )
```

```python
import functools
import math

import jax
import jax.numpy as jnp
import ml_dtypes
import numpy as np
from jax import lax
from jax.experimental import pallas as pl
from jax.experimental.pallas import tpu as pltpu
from jax.sharding import PartitionSpec as P

SECTION_A = 128
MARGIN = 128
FG = 8
MESH = pl.DeviceIdType.MESH
F32 = jnp.float32
BF16 = jnp.bfloat16


def dft_table(length, rotation):
    indices = np.arange(length)
    angles = (indices[:, None] * indices[None, :] % length) * (2.0 * math.pi / length)
    factor = 1.0 / math.sqrt(length)
    rounded = lambda values: values.astype(ml_dtypes.bfloat16).astype(np.float32)
    return rounded(np.cos(angles) * factor), rounded(rotation * np.sin(angles) * factor)


def tables(n, pulses, rows, margin_blocks, block, per_device):
    length = block + MARGIN
    groups = per_device // FG
    freq = np.arange(length).reshape(n, groups, FG).transpose(1, 0, 2)
    real, imag = dft_table(length, -1.0)
    sources = n + margin_blocks
    forward = np.zeros((groups, n, 2, FG, sources, rows), np.float32)
    for s in range(sources):
        first = s * pulses if s < n else block + (s - n) * pulses
        count = min(pulses, (block if s < n else length) - first)
        m = first + np.arange(count)
        wr = real[m][:, freq].transpose(1, 2, 3, 0)
        wi = imag[m][:, freq].transpose(1, 2, 3, 0)
        forward[:, :, 0, :, s, :count] = wr
        forward[:, :, 0, :, s, pulses : pulses + count] = -wi
        forward[:, :, 1, :, s, :count] = wi
        forward[:, :, 1, :, s, pulses : pulses + count] = wr
    forward = forward.reshape(groups, n * 2 * FG, sources * rows)
    real, imag = dft_table(length, 1.0)
    backward = np.zeros((2, block, groups, n, 2, FG), np.float32)
    wr, wi = real[:block][:, freq], imag[:block][:, freq]
    backward[0, :, :, :, 0], backward[0, :, :, :, 1] = wr, -wi
    backward[1, :, :, :, 0], backward[1, :, :, :, 1] = wi, wr
    backward = backward.reshape(2 * block, groups, n * 2 * FG).transpose(1, 0, 2)
    sections = []
    for rotation in (-1.0, 1.0):
        real, imag = dft_table(SECTION_A, rotation)
        sections.append(np.block([[real, -imag], [imag, real]]))
        sections.append(np.block([[real, imag], [-imag, real]]))
    index = np.arange(SECTION_A)
    angles = index[:, None] * index[None, :] * (2.0 * math.pi / SECTION_A**2)
    twiddle = np.stack([np.cos(angles), np.sin(angles)]).astype(np.float32)
    as_bf16 = lambda values: values.astype(ml_dtypes.bfloat16)
    return as_bf16(forward), as_bf16(backward), as_bf16(np.stack(sections)), twiddle


def cos_sin(x):
    h = x * 0.5
    q = h * h
    s = 1.0 / 362880.0
    for c in (-1.0 / 5040.0, 1.0 / 120.0, -1.0 / 6.0, 1.0):
        s = s * q + c
    s = s * h
    k = -1.0 / 3628800.0
    for c in (1.0 / 40320.0, -1.0 / 720.0, 1.0 / 24.0, -0.5, 1.0):
        k = k * q + c
    return 1.0 - 2.0 * s * s, 2.0 * s * k


def kernel(
    n, n_az, margin_blocks, groups, rc,
    echoes, scaling, rng, residual, forward_in, backward_in, sections_in, twiddle_in,
    out,
    wide, narrow, spec_wide, recv_wide, spec, recv2, send3, recv3, ph, sc_t, rg_t, rs_t, xs, total_back,
    forward, backward, sections, twiddle,
    s1, r1, sw, rw, lw, s2, r2, l2, s3, r3, l3, pm, ms, mr, tm,
):
    a, me = lax.axis_index("az"), lax.axis_index("row")
    lane_tiles, w_wide, w_narrow = rc // 128, rc - rc // 4, rc // 4
    half_row = n // 2
    side, place = lax.div(me, half_row), lax.rem(me, half_row)
    order = [(1, 0)]
    for i in range(1, half_row):
        order += [(0, i), (1, i)]
    near = [(0, i) for i in range(1, half_row)]

    def peer(partner):
        other, i = partner
        there = 1 - side if other else side
        return there * half_row + lax.rem(place + i, half_row)

    barrier = pltpu.get_barrier_semaphore()
    for i in order:
        pl.semaphore_signal(barrier, inc=1, device_id={"row": peer(i)}, device_id_type=MESH)

    steps = sorted({1, n_az - 1})
    for step in steps:
        beside = lax.rem(a + step, n_az)
        pl.semaphore_signal(barrier, inc=1, device_id={"az": beside}, device_id_type=MESH)
    pl.semaphore_wait(barrier, n - 1 + len(steps))

    def columns(d):
        return pl.ds(pl.multiple_of(d * rc, 128), rc)

    def piece(d, slot):
        if slot < 2:
            start = (lax.rem(d, half_row) + slot * half_row) * rc
            return pl.ds(pl.multiple_of(start, 128), w_wide)
        return pl.ds(pl.multiple_of(d * rc + w_wide, 128), w_narrow)

    def landing(slot, at):
        return wide.at[slot, at] if slot < 2 else narrow.at[at]

    for slots in ((0, 1), (2,)):
        for i in order:
            d = peer(i)
            for slot in slots:
                pltpu.make_async_remote_copy(
                    src_ref=echoes.at[:, piece(d, slot)], dst_ref=landing(slot, me),
                    send_sem=s1.at[slot], recv_sem=r1.at[slot, me],
                    device_id={"row": d}, device_id_type=MESH,
                ).start()
        for slot in slots:
            pltpu.make_async_copy(
                echoes.at[:, piece(me, slot)], landing(slot, me), r1.at[slot, me]
            ).start()
    loads = [pltpu.make_async_copy(p, ph.at[k], pm.at[k]) for k, p in enumerate((scaling, rng, residual))]
    fixed = ((forward_in, forward), (twiddle_in, twiddle), (sections_in, sections), (backward_in, backward))
    loads += [pltpu.make_async_copy(x, y, tm.at[k]) for k, (x, y) in enumerate(fixed)]
    for k in (0, 3, 1, 2, 4, 5, 6):
        loads[k].start()

    @pl.when(a == n_az - 1)
    def _():
        for j in range(margin_blocks):
            for slot in range(2):
                wide[slot, n + j] = jnp.zeros(wide.shape[2:], BF16)
            narrow[n + j] = jnp.zeros(narrow.shape[1:], BF16)

    def natural_table(k, table):
        loads[k].wait()

        def natural(step, carry):
            pair, d = lax.div(step, n), lax.rem(step, n)
            rows = pl.ds(pl.multiple_of(pair * 2 * FG, 2 * FG), 2 * FG)
            c, s = cos_sin(ph[k, rows, columns(d)].astype(F32))
            for h in range(2):
                table[2 * pair + h, d, 0] = c[h * FG : (h + 1) * FG]
                table[2 * pair + h, d, 1] = s[h * FG : (h + 1) * FG]
            return carry

        lax.fori_loop(0, n * (groups // 2), natural, 0)

    def turned_table():
        loads[1].wait()

        def turn(pair, carry):
            rows = pl.ds(pl.multiple_of(pair * 2 * FG, 2 * FG), 2 * FG)

            def spread(d, inner):
                x = ph[1, rows, columns(d)].astype(F32)
                for j in range(lane_tiles):
                    at = pl.ds(pl.multiple_of((d * lane_tiles + j) * FG, FG), FG)
                    for h in range(2):
                        xs[h, at, :] = x[h * FG : (h + 1) * FG, j * 128 : (j + 1) * 128]
                return inner

            lax.fori_loop(0, n, spread, 0)
            for h in range(2):
                for f in range(FG):
                    c, s = cos_sin(xs[h, pl.ds(f, 128, stride=FG), :].T)
                    rg_t[2 * pair + h, f, 0] = c
                    rg_t[2 * pair + h, f, 1] = s
            return carry

        lax.fori_loop(0, groups // 2, turn, 0)

    def margin_copy(slot):
        return pltpu.make_async_remote_copy(
            src_ref=landing(slot, pl.ds(0, margin_blocks)),
            dst_ref=landing(slot, pl.ds(n, margin_blocks)),
            send_sem=ms.at[slot], recv_sem=mr.at[slot],
            device_id={"az": a - 1}, device_id_type=MESH,
        )

    def pulses_arrived(slots):
        def arrived(slot, s):
            pltpu.make_async_copy(
                echoes.at[:, piece(me, slot)], landing(slot, s), r1.at[slot, s]
            ).wait()

        for slot in slots:
            for s in range(margin_blocks):
                arrived(slot, s)

            @pl.when(a > 0)
            def _(slot=slot):
                margin_copy(slot).start()

        for slot in slots:
            for s in range(margin_blocks, n):
                arrived(slot, s)

            @pl.when(a < n_az - 1)
            def _(slot=slot):
                pltpu.make_async_copy(
                    landing(slot, pl.ds(0, margin_blocks)), landing(slot, pl.ds(n, margin_blocks)),
                    mr.at[slot],
                ).wait()

    def send_group(source, target, at, send_sem, recv_sem, local_sem):
        for i in order:
            d = peer(i)
            pltpu.make_async_remote_copy(
                src_ref=source.at[(*at, d)], dst_ref=target.at[(*at, me)], send_sem=send_sem.at[at],
                recv_sem=recv_sem.at[at], device_id={"row": d}, device_id_type=MESH,
            ).start()
        pltpu.make_async_copy(
            source.at[(*at, me)], target.at[(*at, me)], local_sem.at[at]
        ).start()

    def group_wait(source, target, at, sem):
        some = pl.ds(0, n - 1)
        pltpu.make_async_copy(source.at[(*at, some)], target.at[(*at, some)], sem.at[at]).wait()

    def group_arrived(source, target, at, recv_sem, local_sem):
        group_wait(source, target, at, recv_sem)
        pltpu.make_async_copy(source.at[(*at, me)], target.at[(*at, me)], local_sem.at[at]).wait()

    depth = narrow.shape[0] * narrow.shape[1]
    rows_half = half_row * 2 * FG

    def azimuth_wide():
        pulses_arrived((0, 1))
        mine = pl.ds(pl.multiple_of(side * rows_half, 16), rows_half)
        for slot in range(2):
            total = jnp.dot(
                forward[:, mine, :].reshape(groups * rows_half, depth),
                wide[slot].reshape(depth, w_wide), preferred_element_type=F32,
            )
            for g in range(groups):
                rows = total[g * rows_half : (g + 1) * rows_half].astype(BF16)
                spec_wide[g, :, slot] = rows.reshape(half_row, 2 * FG, w_wide)

        def send(g, carry):
            for i in near:
                d = peer(i)
                pltpu.make_async_remote_copy(
                    src_ref=spec_wide.at[g, lax.rem(d, half_row)], dst_ref=recv_wide.at[g, place],
                    send_sem=sw.at[g], recv_sem=rw.at[g],
                    device_id={"row": d}, device_id_type=MESH,
                ).start()
            pltpu.make_async_copy(
                spec_wide.at[g, place], recv_wide.at[g, place], lw.at[g]
            ).start()
            return carry

        lax.fori_loop(0, groups, send, 0)

    def wide_wait(g, sem):
        some = pl.ds(0, half_row - 1)
        pltpu.make_async_copy(spec_wide.at[g, some], recv_wide.at[g, some], sem.at[g]).wait()

    def azimuth_narrow():
        pulses_arrived((2,))

        def azimuth(g, carry):
            total = jnp.dot(
                forward[g], narrow[...].reshape(depth, w_narrow), preferred_element_type=F32
            )
            spec[g] = total.astype(BF16).reshape(n, 2 * FG, w_narrow)
            send_group(spec, recv2, (g,), s2, r2, l2)
            return carry

        lax.fori_loop(0, groups, azimuth, 0)

    natural_table(0, sc_t)
    loads[3].wait()
    turned_table()
    azimuth_wide()
    azimuth_narrow()
    natural_table(2, rs_t)
    for k in (4, 5, 6):
        loads[k].wait()

    def part(values, f):
        return values[:, f * 128 : (f + 1) * 128]

    def range_group(g, carry):
        wide_wait(g, rw)
        pltpu.make_async_copy(spec_wide.at[g, place], recv_wide.at[g, place], lw.at[g]).wait()
        group_arrived(spec, recv2, (g,), r2, l2)

        def scale(d, inner):
            first = recv_wide[g, lax.rem(d, half_row), lax.div(d, half_row)]
            block = jnp.concatenate([first, recv2[g, d]], axis=1).astype(F32)
            re, im = block[:FG], block[FG:]
            c, s = sc_t[g, d, 0], sc_t[g, d, 1]
            x, y = re * c - im * s, re * s + im * c
            for j in range(lane_tiles):
                at = pl.ds(pl.multiple_of((d * lane_tiles + j) * FG, FG), FG)
                xs[0, at, :] = part(x, j)
                xs[1, at, :] = part(y, j)
            return inner

        lax.fori_loop(0, n, scale, 0)
        tc, ts = twiddle[0], twiddle[1]
        v = jnp.concatenate(
            [
                jnp.concatenate(
                    [xs[c, pl.ds(f, 128, stride=FG), :].astype(BF16) for f in range(FG)], axis=1
                )
                for c in range(2)
            ],
            axis=0,
        )
        y = jnp.dot(sections[0], v, preferred_element_type=F32)
        half = []
        for f in range(FG):
            re, im = part(y[:128], f), part(y[128:], f)
            half.append(jnp.concatenate([re * tc + im * ts, im * tc - re * ts], axis=1).astype(BF16))
        z = jnp.dot(jnp.concatenate(half, axis=0), sections[1], preferred_element_type=F32)
        squeezed = []
        for f in range(FG):
            rows = z[f * 128 : (f + 1) * 128]
            re, im = rows[:, :128], rows[:, 128:]
            c, s = rg_t[g, f, 0], rg_t[g, f, 1]
            squeezed.append(jnp.concatenate([re * c - im * s, re * s + im * c], axis=1).astype(BF16))
        u = jnp.dot(jnp.concatenate(squeezed, axis=0), sections[3], preferred_element_type=F32)
        reals, imags = [], []
        for f in range(FG):
            rows = u[f * 128 : (f + 1) * 128]
            re, im = rows[:, :128], rows[:, 128:]
            reals.append((re * tc - im * ts).astype(BF16))
            imags.append((re * ts + im * tc).astype(BF16))
        q = jnp.concatenate(
            [jnp.concatenate(reals, axis=1), jnp.concatenate(imags, axis=1)], axis=0
        )
        w = jnp.dot(sections[2], q, preferred_element_type=F32)
        for f in range(FG):
            xs[0, pl.ds(f, 128, stride=FG), :] = part(w[:128], f)
            xs[1, pl.ds(f, 128, stride=FG), :] = part(w[128:], f)

        def finish(d, inner):
            res, ims = [], []
            for j in range(lane_tiles):
                at = pl.ds(pl.multiple_of((d * lane_tiles + j) * FG, FG), FG)
                res.append(xs[0, at, :])
                ims.append(xs[1, at, :])
            re, im = jnp.concatenate(res, axis=1), jnp.concatenate(ims, axis=1)
            c, s = rs_t[g, d, 0], rs_t[g, d, 1]
            send3[g, d] = jnp.concatenate([re * c - im * s, re * s + im * c], axis=0).astype(BF16)
            return inner

        lax.fori_loop(0, n, finish, 0)
        send_group(send3, recv3, (g,), s3, r3, l3)
        return carry

    lax.fori_loop(0, groups, range_group, 0)

    for g in range(groups):
        group_arrived(send3, recv3, (g,), r3, l3)
        term = jnp.dot(
            backward[g], recv3[g].reshape(n * 2 * FG, rc), preferred_element_type=F32
        )
        if g > 0:
            term = total_back[...] + term
        if g < groups - 1:
            total_back[...] = term
        else:
            out[...] = term.astype(BF16)

    for g in range(groups):
        wide_wait(g, sw)
        group_wait(spec, recv2, (g,), s2)
        group_wait(send3, recv3, (g,), s3)
    some = pl.ds(0, n - 1)
    for slot in range(3):
        pltpu.make_async_copy(landing(slot, some), landing(slot, some), s1.at[slot]).wait()

        @pl.when(a > 0)
        def _(slot=slot):
            margin_copy(slot).wait_send()


def on_device(n_az, n, echoes, scaling_phase, range_phase, residual_phase):
    _, pulses, length = echoes.shape
    per_device = scaling_phase.shape[0]
    rc = length // n
    block = pulses * n
    rows = -(-2 * pulses // 16) * 16
    margin_blocks = -(-MARGIN // pulses)
    groups = per_device // FG
    stacked = echoes.reshape(2 * pulses, length)
    if rows > 2 * pulses:
        stacked = jnp.pad(stacked, ((0, rows - 2 * pulses), (0, 0)))
    forward, backward, sections, twiddle = tables(n, pulses, rows, margin_blocks, block, per_device)
    anywhere = pl.BlockSpec(memory_space=pl.ANY)
    vmem = pl.BlockSpec(memory_space=pltpu.VMEM)
    exchange = pltpu.VMEM((groups, n, 2 * FG, rc), BF16)
    w_narrow = rc // 4
    w_wide = rc - w_narrow
    sources = n + margin_blocks
    narrow_groups = pltpu.VMEM((groups, n, 2 * FG, w_narrow), BF16)
    wide_groups = pltpu.VMEM((groups, n // 2, 2, 2 * FG, w_wide), BF16)
    dma = pltpu.SemaphoreType.DMA
    result = pl.pallas_call(
        functools.partial(kernel, n, n_az, margin_blocks, groups, rc),
        out_shape=jax.ShapeDtypeStruct((2 * block, rc), BF16),
        in_specs=[anywhere] * 8,
        out_specs=vmem,
        scratch_shapes=[
            pltpu.VMEM((2, sources, rows, w_wide), BF16),
            pltpu.VMEM((sources, rows, w_narrow), BF16),
            wide_groups, wide_groups, narrow_groups, narrow_groups, exchange, exchange,
            pltpu.VMEM((3, per_device, length), BF16),
            pltpu.VMEM((groups, n, 2, FG, rc), F32),
            pltpu.VMEM((groups, FG, 2, 128, 128), F32),
            pltpu.VMEM((groups, n, 2, FG, rc), F32),
            pltpu.VMEM((2, 128 * FG, 128), F32),
            pltpu.VMEM((2 * block, rc), F32),
            *[pltpu.VMEM(t.shape, t.dtype) for t in (forward, backward, sections, twiddle)],
            dma((3,)), dma((3, n)), *[dma((groups,))] * 9,
            dma((3,)), dma((3,)), dma((3,)), dma((4,)),
        ],
        compiler_params=pltpu.CompilerParams(
            collective_id=0, has_side_effects=True, vmem_limit_bytes=56 * 1024 * 1024
        ),
    )(
        stacked, scaling_phase, range_phase, residual_phase,
        jnp.asarray(forward), jnp.asarray(backward), jnp.asarray(sections), jnp.asarray(twiddle),
    )
    return result.reshape(2, block, rc)


def solution(mesh):
    placed = (P(None, ("az", "row"), None), P("row", None), P("row", None), P("row", None))
    return jax.shard_map(
        functools.partial(on_device, mesh.shape["az"], mesh.shape["row"]),
        mesh=mesh, in_specs=placed, out_specs=P(None, "az", "row"), check_vma=False,
    )
```

```python
import functools
import math

import jax
import jax.numpy as jnp
import ml_dtypes
import numpy as np
from jax import lax
from jax.experimental import pallas as pl
from jax.experimental.pallas import tpu as pltpu
from jax.sharding import PartitionSpec as P

SECTION_A = 128
MARGIN = 128
FG = 8
CHUNKS = 2
MESH = pl.DeviceIdType.MESH
F32 = jnp.float32
BF16 = jnp.bfloat16


def dft_table(length, rotation):
    indices = np.arange(length)
    angles = (indices[:, None] * indices[None, :] % length) * (2.0 * math.pi / length)
    factor = 1.0 / math.sqrt(length)
    rounded = lambda values: values.astype(ml_dtypes.bfloat16).astype(np.float32)
    return rounded(np.cos(angles) * factor), rounded(rotation * np.sin(angles) * factor)


def tables(n, pulses, rows, margin_blocks, block, per_device):
    length = block + MARGIN
    groups = per_device // FG
    freq = np.arange(length).reshape(n, groups, FG).transpose(1, 0, 2)
    real, imag = dft_table(length, -1.0)
    sources = n + margin_blocks
    forward = np.zeros((groups, n, 2, FG, sources, rows), np.float32)
    for s in range(sources):
        first = s * pulses if s < n else block + (s - n) * pulses
        count = min(pulses, (block if s < n else length) - first)
        m = first + np.arange(count)
        wr = real[m][:, freq].transpose(1, 2, 3, 0)
        wi = imag[m][:, freq].transpose(1, 2, 3, 0)
        forward[:, :, 0, :, s, :count] = wr
        forward[:, :, 0, :, s, pulses : pulses + count] = -wi
        forward[:, :, 1, :, s, :count] = wi
        forward[:, :, 1, :, s, pulses : pulses + count] = wr
    forward = forward.reshape(groups, n * 2 * FG, sources * rows)
    real, imag = dft_table(length, 1.0)
    backward = np.zeros((2, block, groups, n, 2, FG), np.float32)
    wr, wi = real[:block][:, freq], imag[:block][:, freq]
    backward[0, :, :, :, 0], backward[0, :, :, :, 1] = wr, -wi
    backward[1, :, :, :, 0], backward[1, :, :, :, 1] = wi, wr
    backward = backward.reshape(2 * block, groups, n * 2 * FG).transpose(1, 0, 2)
    sections = []
    for rotation in (-1.0, 1.0):
        real, imag = dft_table(SECTION_A, rotation)
        sections.append(np.block([[real, -imag], [imag, real]]))
        sections.append(np.block([[real, imag], [-imag, real]]))
    index = np.arange(SECTION_A)
    angles = index[:, None] * index[None, :] * (2.0 * math.pi / SECTION_A**2)
    twiddle = np.stack([np.cos(angles), np.sin(angles)]).astype(np.float32)
    as_bf16 = lambda values: values.astype(ml_dtypes.bfloat16)
    return as_bf16(forward), as_bf16(backward), as_bf16(np.stack(sections)), twiddle


def cos_sin(x):
    h = x * 0.5
    q = h * h
    s = 1.0 / 362880.0
    for c in (-1.0 / 5040.0, 1.0 / 120.0, -1.0 / 6.0, 1.0):
        s = s * q + c
    s = s * h
    k = -1.0 / 3628800.0
    for c in (1.0 / 40320.0, -1.0 / 720.0, 1.0 / 24.0, -0.5, 1.0):
        k = k * q + c
    return 1.0 - 2.0 * s * s, 2.0 * s * k


def kernel(
    n, n_az, margin_blocks, groups, rc,
    echoes, scaling, rng, residual, forward_in, backward_in, sections_in, twiddle_in,
    out,
    recv1, spec, recv2, send3, recv3, ph, sc_t, rg_t, rs_t, xs, total_back,
    forward, backward, sections, twiddle,
    s1, r1, s2, r2, l2, s3, r3, l3, pm, ms, mr, tm,
):
    a, me = lax.axis_index("az"), lax.axis_index("row")
    lane_tiles, cw = rc // 128, rc // CHUNKS
    half_row = n // 2
    side, place = lax.div(me, half_row), lax.rem(me, half_row)
    order = [(1, 0)]
    for i in range(1, half_row):
        order += [(0, i), (1, i)]

    def peer(partner):
        other, i = partner
        there = 1 - side if other else side
        return there * half_row + lax.rem(place + i, half_row)

    barrier = pltpu.get_barrier_semaphore()
    for i in order:
        pl.semaphore_signal(barrier, inc=1, device_id={"row": peer(i)}, device_id_type=MESH)

    steps = sorted({1, n_az - 1})
    for step in steps:
        beside = lax.rem(a + step, n_az)
        pl.semaphore_signal(barrier, inc=1, device_id={"az": beside}, device_id_type=MESH)
    pl.semaphore_wait(barrier, n - 1 + len(steps))

    def columns(d):
        return pl.ds(pl.multiple_of(d * rc, 128), rc)

    def chunk_columns(d, ch):
        return pl.ds(pl.multiple_of(d * rc + ch * cw, 128), cw)

    for ch in range(CHUNKS):
        for i in order:
            d = peer(i)
            pltpu.make_async_remote_copy(
                src_ref=echoes.at[:, chunk_columns(d, ch)], dst_ref=recv1.at[ch, me],
                send_sem=s1.at[ch], recv_sem=r1.at[ch, me],
                device_id={"row": d}, device_id_type=MESH,
            ).start()
        pltpu.make_async_copy(
            echoes.at[:, chunk_columns(me, ch)], recv1.at[ch, me], r1.at[ch, me]
        ).start()
    loads = [pltpu.make_async_copy(p, ph.at[k], pm.at[k]) for k, p in enumerate((scaling, rng, residual))]
    fixed = ((forward_in, forward), (twiddle_in, twiddle), (sections_in, sections), (backward_in, backward))
    loads += [pltpu.make_async_copy(x, y, tm.at[k]) for k, (x, y) in enumerate(fixed)]
    for k in (0, 3, 1, 2, 4, 5, 6):
        loads[k].start()

    @pl.when(a == n_az - 1)
    def _():
        for ch in range(CHUNKS):
            for j in range(margin_blocks):
                recv1[ch, n + j] = jnp.zeros(recv1.shape[2:], BF16)

    def natural_table(k, table, pair):
        def natural(d, carry):
            rows = pl.ds(pl.multiple_of(pair * 2 * FG, 2 * FG), 2 * FG)
            c, s = cos_sin(ph[k, rows, columns(d)].astype(F32))
            for h in range(2):
                table[2 * pair + h, d, 0] = c[h * FG : (h + 1) * FG]
                table[2 * pair + h, d, 1] = s[h * FG : (h + 1) * FG]
            return carry

        lax.fori_loop(0, n, natural, 0)

    def turned_table():
        loads[1].wait()

        def turn(pair, carry):
            rows = pl.ds(pl.multiple_of(pair * 2 * FG, 2 * FG), 2 * FG)

            def spread(d, inner):
                x = ph[1, rows, columns(d)].astype(F32)
                for j in range(lane_tiles):
                    at = pl.ds(pl.multiple_of((d * lane_tiles + j) * FG, FG), FG)
                    for h in range(2):
                        xs[h, at, :] = x[h * FG : (h + 1) * FG, j * 128 : (j + 1) * 128]
                return inner

            lax.fori_loop(0, n, spread, 0)
            for h in range(2):
                for f in range(FG):
                    c, s = cos_sin(xs[h, pl.ds(f, 128, stride=FG), :].T)
                    rg_t[2 * pair + h, f, 0] = c
                    rg_t[2 * pair + h, f, 1] = s
            return carry

        lax.fori_loop(0, groups // 2, turn, 0)

    def arrived(ch, s):
        pltpu.make_async_copy(echoes.at[:, pl.ds(0, cw)], recv1.at[ch, s], r1.at[ch, s]).wait()

    def margin_copy(ch):
        return pltpu.make_async_remote_copy(
            src_ref=recv1.at[ch, pl.ds(0, margin_blocks)],
            dst_ref=recv1.at[ch, pl.ds(n, margin_blocks)],
            send_sem=ms.at[ch], recv_sem=mr.at[ch],
            device_id={"az": a - 1}, device_id_type=MESH,
        )

    def send_group(source, target, at, send_sem, recv_sem, local_sem):
        for i in order:
            d = peer(i)
            pltpu.make_async_remote_copy(
                src_ref=source.at[(*at, d)], dst_ref=target.at[(*at, me)], send_sem=send_sem.at[at],
                recv_sem=recv_sem.at[at], device_id={"row": d}, device_id_type=MESH,
            ).start()
        pltpu.make_async_copy(
            source.at[(*at, me)], target.at[(*at, me)], local_sem.at[at]
        ).start()

    def group_wait(source, target, at, sem):
        some = pl.ds(0, n - 1)
        pltpu.make_async_copy(source.at[(*at, some)], target.at[(*at, some)], sem.at[at]).wait()

    def group_arrived(source, target, at, recv_sem, local_sem):
        group_wait(source, target, at, recv_sem)
        pltpu.make_async_copy(source.at[(*at, me)], target.at[(*at, me)], local_sem.at[at]).wait()

    depth = recv1.shape[1] * recv1.shape[2]

    def azimuth_chunk(ch):
        for s in range(margin_blocks):
            arrived(ch, s)

        @pl.when(a > 0)
        def _():
            margin_copy(ch).start()

        for s in range(margin_blocks, n):
            arrived(ch, s)

        @pl.when(a < n_az - 1)
        def _():
            pltpu.make_async_copy(
                recv1.at[ch, pl.ds(0, margin_blocks)], recv1.at[ch, pl.ds(n, margin_blocks)],
                mr.at[ch],
            ).wait()

        def azimuth(g, carry):
            total = jnp.dot(
                forward[g], recv1[ch].reshape(depth, cw), preferred_element_type=F32
            )
            spec[g, ch] = total.astype(BF16).reshape(n, 2 * FG, cw)

            @pl.when((g == 0) if ch == 0 else (g > 0))
            def _():
                send_group(spec, recv2, (g, 0), s2, r2, l2)

            if ch == 1:
                send_group(spec, recv2, (g, 1), s2, r2, l2)
            return carry

        lax.fori_loop(0, groups, azimuth, 0)

    loads[0].wait()
    for pair in range(groups // 2):
        natural_table(0, sc_t, pair)
    loads[3].wait()
    azimuth_chunk(0)
    turned_table()
    azimuth_chunk(1)
    for k in (2, 4, 5, 6):
        loads[k].wait()

    def part(values, f):
        return values[:, f * 128 : (f + 1) * 128]

    def range_group(g, carry):
        for ch in range(CHUNKS):
            group_arrived(spec, recv2, (g, ch), r2, l2)

        def scale(d, inner):
            block = jnp.concatenate([recv2[g, ch, d] for ch in range(CHUNKS)], axis=1).astype(F32)
            re, im = block[:FG], block[FG:]
            c, s = sc_t[g, d, 0], sc_t[g, d, 1]
            x, y = re * c - im * s, re * s + im * c
            for j in range(lane_tiles):
                at = pl.ds(pl.multiple_of((d * lane_tiles + j) * FG, FG), FG)
                xs[0, at, :] = part(x, j)
                xs[1, at, :] = part(y, j)
            return inner

        lax.fori_loop(0, n, scale, 0)
        tc, ts = twiddle[0], twiddle[1]
        v = jnp.concatenate(
            [
                jnp.concatenate(
                    [xs[c, pl.ds(f, 128, stride=FG), :].astype(BF16) for f in range(FG)], axis=1
                )
                for c in range(2)
            ],
            axis=0,
        )
        y = jnp.dot(sections[0], v, preferred_element_type=F32)
        half = []
        for f in range(FG):
            re, im = part(y[:128], f), part(y[128:], f)
            half.append(jnp.concatenate([re * tc + im * ts, im * tc - re * ts], axis=1).astype(BF16))
        z = jnp.dot(jnp.concatenate(half, axis=0), sections[1], preferred_element_type=F32)
        squeezed = []
        for f in range(FG):
            rows = z[f * 128 : (f + 1) * 128]
            re, im = rows[:, :128], rows[:, 128:]
            c, s = rg_t[g, f, 0], rg_t[g, f, 1]
            squeezed.append(jnp.concatenate([re * c - im * s, re * s + im * c], axis=1).astype(BF16))
        u = jnp.dot(jnp.concatenate(squeezed, axis=0), sections[3], preferred_element_type=F32)
        reals, imags = [], []
        for f in range(FG):
            rows = u[f * 128 : (f + 1) * 128]
            re, im = rows[:, :128], rows[:, 128:]
            reals.append((re * tc - im * ts).astype(BF16))
            imags.append((re * ts + im * tc).astype(BF16))
        q = jnp.concatenate(
            [jnp.concatenate(reals, axis=1), jnp.concatenate(imags, axis=1)], axis=0
        )
        w = jnp.dot(sections[2], q, preferred_element_type=F32)
        for f in range(FG):
            xs[0, pl.ds(f, 128, stride=FG), :] = part(w[:128], f)
            xs[1, pl.ds(f, 128, stride=FG), :] = part(w[128:], f)

        def finish(d, inner):
            res, ims = [], []
            for j in range(lane_tiles):
                at = pl.ds(pl.multiple_of((d * lane_tiles + j) * FG, FG), FG)
                res.append(xs[0, at, :])
                ims.append(xs[1, at, :])
            re, im = jnp.concatenate(res, axis=1), jnp.concatenate(ims, axis=1)
            c, s = rs_t[g, d, 0], rs_t[g, d, 1]
            send3[g, d] = jnp.concatenate([re * c - im * s, re * s + im * c], axis=0).astype(BF16)
            return inner

        lax.fori_loop(0, n, finish, 0)
        send_group(send3, recv3, (g,), s3, r3, l3)
        return carry

    def range_pair(pair, carry):
        natural_table(2, rs_t, pair)
        return lax.fori_loop(2 * pair, 2 * pair + 2, range_group, carry)

    lax.fori_loop(0, groups // 2, range_pair, 0)

    for g in range(groups):
        group_arrived(send3, recv3, (g,), r3, l3)
        term = jnp.dot(
            backward[g], recv3[g].reshape(n * 2 * FG, rc), preferred_element_type=F32
        )
        if g > 0:
            term = total_back[...] + term
        if g < groups - 1:
            total_back[...] = term
        else:
            out[...] = term.astype(BF16)

    for g in range(groups):
        for ch in range(CHUNKS):
            group_wait(spec, recv2, (g, ch), s2)
        group_wait(send3, recv3, (g,), s3)
    some = pl.ds(0, n - 1)
    for ch in range(CHUNKS):
        pltpu.make_async_copy(recv1.at[ch, some], recv1.at[ch, some], s1.at[ch]).wait()

        @pl.when(a > 0)
        def _(ch=ch):
            margin_copy(ch).wait_send()


def on_device(n_az, n, echoes, scaling_phase, range_phase, residual_phase):
    _, pulses, length = echoes.shape
    per_device = scaling_phase.shape[0]
    rc = length // n
    block = pulses * n
    rows = -(-2 * pulses // 16) * 16
    margin_blocks = -(-MARGIN // pulses)
    groups = per_device // FG
    stacked = echoes.reshape(2 * pulses, length)
    if rows > 2 * pulses:
        stacked = jnp.pad(stacked, ((0, rows - 2 * pulses), (0, 0)))
    forward, backward, sections, twiddle = tables(n, pulses, rows, margin_blocks, block, per_device)
    anywhere = pl.BlockSpec(memory_space=pl.ANY)
    vmem = pl.BlockSpec(memory_space=pltpu.VMEM)
    exchange = pltpu.VMEM((groups, n, 2 * FG, rc), BF16)
    chunked = pltpu.VMEM((groups, CHUNKS, n, 2 * FG, rc // CHUNKS), BF16)
    dma = pltpu.SemaphoreType.DMA
    result = pl.pallas_call(
        functools.partial(kernel, n, n_az, margin_blocks, groups, rc),
        out_shape=jax.ShapeDtypeStruct((2 * block, rc), BF16),
        in_specs=[anywhere] * 8,
        out_specs=vmem,
        scratch_shapes=[
            pltpu.VMEM((CHUNKS, n + margin_blocks, rows, rc // CHUNKS), BF16),
            chunked, chunked, exchange, exchange,
            pltpu.VMEM((3, per_device, length), BF16),
            pltpu.VMEM((groups, n, 2, FG, rc), F32),
            pltpu.VMEM((groups, FG, 2, 128, 128), F32),
            pltpu.VMEM((groups, n, 2, FG, rc), F32),
            pltpu.VMEM((2, 128 * FG, 128), F32),
            pltpu.VMEM((2 * block, rc), F32),
            *[pltpu.VMEM(t.shape, t.dtype) for t in (forward, backward, sections, twiddle)],
            dma((CHUNKS,)), dma((CHUNKS, n)),
            dma((groups, CHUNKS)), dma((groups, CHUNKS)), dma((groups, CHUNKS)),
            dma((groups,)), dma((groups,)), dma((groups,)),
            dma((3,)), dma((CHUNKS,)), dma((CHUNKS,)), dma((4,)),
        ],
        compiler_params=pltpu.CompilerParams(
            collective_id=0, has_side_effects=True, vmem_limit_bytes=56 * 1024 * 1024
        ),
    )(
        stacked, scaling_phase, range_phase, residual_phase,
        jnp.asarray(forward), jnp.asarray(backward), jnp.asarray(sections), jnp.asarray(twiddle),
    )
    return result.reshape(2, block, rc)


def solution(mesh):
    placed = (P(None, ("az", "row"), None), P("row", None), P("row", None), P("row", None))
    return jax.shard_map(
        functools.partial(on_device, mesh.shape["az"], mesh.shape["row"]),
        mesh=mesh, in_specs=placed, out_specs=P(None, "az", "row"), check_vma=False,
    )
```
